32 devices in a mesh: tok: 4 (over z), row: 4 (over y, core), col: 2 (over x).
Axes of the slice: x: 2, y: 2, z: 4, core: 2. Of those that a mesh axis runs over, the one named last changes fastest.
Arguments:
- activations: bfloat16 [1024, 8192], P('tok', 'row'), may hold values from -8 to 8
- gradients: bfloat16 [1024, 8192], P('tok', 'col'), may hold values from -8 to 8
- act_basis: bfloat16 [8192, 8192], P('row', ('tok', 'col')), may hold values from -1 to 1
- grad_basis: bfloat16 [8192, 8192], P('col', 'row'), may hold values from -1 to 1
- eigen_noise: float32 [8192, 8192], P('row', ('tok', 'col')), may hold values from -6 to 6
Outputs:
- scales: float32 [8192, 8192], P('row', ('tok', 'col'))
- output_shift: bfloat16 [1024, 8192], P('tok', 'col')
The draws below stay inside these ranges and needn't reach their ends.
All inputs are finite; a program needn't handle non-finite values.
Results may differ from the reference program's by a relative error of at most 0.0064.
Values may be sent and summed in bfloat16 or wider, within the bound.
A program may use at most 128 MiB of HBM per device.

```python
import math
import jax
import jax.numpy as jnp
from jax import lax

D = 8192
TOKENS = 1024


def token_scale(key, salt):
    lower = math.log(0.9)
    upper = math.log(1.1)
    spread = jax.random.uniform(jax.random.fold_in(key, salt), (TOKENS, 1), jnp.float32, lower, upper)
    return jnp.exp(spread)


def column_scale(key):
    spread = jax.random.uniform(key, (1, D), jnp.float32, math.log(0.5), math.log(2.0))
    return jnp.exp(spread)


def unit_values(key, shape):
    return jnp.clip(jax.random.normal(key, shape, jnp.float32), -4.0, 4.0)


def draw_activations(key, part):
    values = unit_values(jax.random.fold_in(key, 21), (TOKENS, D))
    return (token_scale(key, 7) * values).astype(jnp.bfloat16)


def draw_gradients(key, part):
    values = unit_values(jax.random.fold_in(key, 22), (TOKENS, D))
    return (token_scale(key, 8) * values).astype(jnp.bfloat16)


def draw_act_basis(key, part):
    values = unit_values(jax.random.fold_in(key, 41), (D, D))
    factor = column_scale(jax.random.fold_in(key, 31))
    return (factor * values / math.sqrt(D)).astype(jnp.bfloat16)


def draw_grad_basis(key, part):
    values = unit_values(jax.random.fold_in(key, 42), (D, D))
    factor = column_scale(jax.random.fold_in(key, 32))
    return (factor * values / math.sqrt(D)).astype(jnp.bfloat16)


def shard_levels(key, extent, split, smallest, largest):
    factor_of = 1.0
    for dim, shards_of in split:
        draws = jax.random.uniform(jax.random.fold_in(jax.random.fold_in(key, 6), dim), (shards_of,), jnp.float32, smallest / len(split), largest / len(split))
        factor_of = factor_of * jnp.repeat(jnp.exp(draws), extent[dim] // shards_of).reshape((-1,) + (1,) * (len(extent) - 1 - dim))
    return factor_of


def noise(stream_key, extent, deviation, limit, cuts=(), kind=jnp.bfloat16):
    drawn = deviation * jax.random.normal(stream_key, extent, jnp.float32)
    if cuts:
        drawn = drawn * shard_levels(stream_key, extent, cuts, -0.22, 0.18)
    return jnp.clip(drawn, -limit, limit).astype(kind)


def setup_inputs(seed: int = 0) -> dict:
    seeds = jax.random.split(jax.random.key(seed), 6)
    return {
        "activations": draw_activations(jax.random.fold_in(seeds[5], 71), 0),
        "gradients": draw_gradients(jax.random.fold_in(seeds[5], 71), 0),
        "act_basis": draw_act_basis(jax.random.fold_in(seeds[5], 71), 0),
        "grad_basis": draw_grad_basis(jax.random.fold_in(seeds[5], 71), 0),
        "eigen_noise": noise(seeds[4], (D, D), 1.0, 6.0, ((0, 4), (1, 8)), jnp.float32),
    }


damping = 0.1

def contract(former, latter, former_dim, latter_dim):
    return lax.dot_general(former, latter, (((former_dim,), (latter_dim,)), ((), ())), preferred_element_type=jnp.float32)

def reference(activations, gradients, act_basis, grad_basis, eigen_noise):
    act_proj = contract(activations, act_basis, 1, 0)
    grad_proj = contract(gradients, grad_basis, 1, 0)
    act_sq = (act_proj * act_proj).astype(jnp.bfloat16)
    grad_sq = (grad_proj * grad_proj).astype(jnp.bfloat16)
    scales = contract(grad_sq, act_sq, 0, 0) / TOKENS
    scaled = (eigen_noise * lax.rsqrt(TOKENS * (scales + damping))).astype(jnp.bfloat16)
    act_half = act_proj.astype(jnp.bfloat16)
    hidden = contract(act_half, scaled, 1, 1).astype(jnp.bfloat16)
    output_shift = contract(hidden, grad_basis, 1, 1).astype(jnp.bfloat16)
    return (scales, output_shift)
```

```python
import jax
import jax.numpy as jnp
from jax import lax
from jax.sharding import PartitionSpec as P

damping = 0.1


def contract(former, latter, former_dim, latter_dim):
    return lax.dot_general(
        former,
        latter,
        (((former_dim,), (latter_dim,)), ((), ())),
        preferred_element_type=jnp.float32,
    )


def shards(activations, gradients, act_basis, grad_basis, eigen_noise):
    half = jnp.bfloat16
    token_count = activations.shape[0] * lax.axis_size("tok")
    acts = lax.all_gather(activations, "tok", axis=0, tiled=True)
    grad_part = contract(gradients, grad_basis, 1, 0).astype(half)
    grad_proj = lax.psum(grad_part, "col").astype(jnp.float32)
    grad_sq = (grad_proj * grad_proj).astype(half)
    grad_all = lax.all_gather(grad_sq, "tok", axis=0, tiled=True)
    act_wide = lax.psum(contract(acts, act_basis, 1, 0), "row")
    act_half = act_wide.astype(half)
    act_sq = (act_wide * act_wide).astype(half)
    scales = contract(grad_all, act_sq, 0, 0) / token_count
    scaled = (eigen_noise * lax.rsqrt(token_count * (scales + damping))).astype(half)
    hidden_part = contract(act_half, scaled, 1, 1).astype(half)
    hidden_part = lax.psum_scatter(hidden_part, "tok", scatter_dimension=0, tiled=True)
    hidden = lax.psum(hidden_part, "col")
    output_part = contract(hidden, grad_basis, 1, 1).astype(half)
    output_shift = lax.psum(output_part, "row")
    return (scales, output_shift)


def solution(mesh):
    in_specs = (
        P("tok", "row"),
        P("tok", "col"),
        P("row", ("tok", "col")),
        P("col", "row"),
        P("row", ("tok", "col")),
    )
    out_specs = (P("row", ("tok", "col")), P("tok", "col"))
    return jax.shard_map(shards, mesh=mesh, in_specs=in_specs, out_specs=out_specs, check_vma=False)
```

```python
import functools

import jax
import jax.numpy as jnp
from jax import lax
from jax.experimental import pallas as pl
from jax.experimental.pallas import tpu as pltpu
from jax.sharding import PartitionSpec as P

damping = 0.1
half = jnp.bfloat16
wide = jnp.float32
MESH = pl.DeviceIdType.MESH
VMEM_BYTES = 60 * 1024 * 1024


def contract(former, latter, former_dim, latter_dim):
    return lax.dot_general(
        former,
        latter,
        (((former_dim,), (latter_dim,)), ((), ())),
        preferred_element_type=jnp.float32,
    )


def remote(src, dst, send_sem, recv_sem, where):
    return pltpu.make_async_remote_copy(
        src_ref=src, dst_ref=dst, send_sem=send_sem, recv_sem=recv_sem,
        device_id=where, device_id_type=MESH,
    )


def arrived(ref, sem, where):
    remote(ref, ref, sem, sem, where).wait_recv()


def enter(nt, nr, nc):
    t, r, c = (lax.axis_index(a) for a in ("tok", "row", "col"))
    barrier = pltpu.get_barrier_semaphore()
    places = [{"tok": lax.rem(t + nt - 1, nt)}]
    places += [{"col": lax.rem(c + k, nc)} for k in range(1, nc)]
    places += [{"row": lax.rem(r + k, nr)} for k in range(1, nr)]
    for place in places:
        pl.semaphore_signal(barrier, inc=1, device_id=place, device_id_type=MESH)
    pl.semaphore_wait(barrier, len(places))
    return t, r, c


def project_kernel(nt, nr, nc, act_hbm, grad_hbm, ab_hbm, gb_hbm, act_half, grad_all,
                   acts, grads, ab, gb, gpart, gown, grecv, part, precv,
                   l_sem, g_send, g_recv, a_send, a_recv, ax_send, ax_recv,
                   c_send, c_recv, cx_send, cx_recv, rs_send, rs_recv, ag_send, ag_recv):
    R = grads.shape[0]
    Fp, Q = ab.shape[1:]
    Pp = gb.shape[2]
    S = R // nr
    t0, c0 = lax.axis_index("tok"), lax.axis_index("col")
    locals_ = []

    def local(src, dst):
        copy = pltpu.make_async_copy(src, dst, l_sem.at[len(locals_)])
        copy.start()
        locals_.append(copy)
        return copy

    act_in = [local(act_hbm.at[:, pl.ds(k * Fp, Fp)], acts.at[k, t0]) for k in range(nc)]
    grad_in = local(grad_hbm, grads)
    gb_in = []
    for k in range(nc):
        peer = lax.rem(c0 + k + 1, nc)
        gb_in.append(local(gb_hbm.at[:, pl.ds(pl.multiple_of(peer * Pp, 128), Pp)], gb.at[k]))
    ab_in = [local(ab_hbm.at[pl.ds(k * Fp, Fp), :], ab.at[k]) for k in range(nc)]

    t, r, c = enter(nt, nr, nc)
    right = {"tok": lax.rem(t + 1, nt)}
    cols = [lax.rem(c + k, nc) for k in range(1, nc)]
    rows = [lax.rem(r + k, nr) for k in range(1, nr)]
    sent = []

    def send(*args):
        copy = remote(*args)
        copy.start()
        sent.append(copy)

    def tok_block(s):
        return lax.rem(t - s + nt, nt)

    def ring(buf, s, send_sem, recv_sem):
        piece = buf.at[c, tok_block(s)]
        send(piece, piece, send_sem.at[s], recv_sem.at[s], right)

    def spread(buf, s, slot, send_sem, recv_sem):
        piece = buf.at[c, tok_block(s)]
        for k, peer in enumerate(cols):
            send(piece, piece, send_sem.at[slot, k], recv_sem.at[slot, c], {"col": peer})

    def ring_recv(buf, s, send_sem, recv_sem, x_send, x_recv):
        arrived(buf.at[c, tok_block(s + 1)], recv_sem.at[s], right)
        if s < nt - 2:
            ring(buf, s + 1, send_sem, recv_sem)
        spread(buf, s + 1, s, x_send, x_recv)

    for copy in act_in:
        copy.wait()
    ring(acts, 0, a_send, a_recv)

    W = min(256, Pp)
    grad_in.wait()
    for k, peer in enumerate(cols):
        gb_in[k].wait()

        @pl.loop(0, Pp // W)
        def _(j, k=k, peer=peer):
            at = pl.ds(pl.multiple_of(j * W, W), W)
            gpart[peer, :, at] = contract(grads[...], gb[k, :, at], 1, 0).astype(half)

        send(gpart.at[peer], grecv.at[c], g_send.at[k], g_recv.at[c], {"col": peer})
    ring_recv(acts, 0, a_send, a_recv, ax_send, ax_recv)
    gb_in[nc - 1].wait()

    @pl.loop(0, Pp // W)
    def _(j):
        at = pl.ds(pl.multiple_of(j * W, W), W)
        gown[:, at] = contract(grads[...], gb[nc - 1, :, at], 1, 0)

    V = min(256, Q)

    def act_block(u):
        b = tok_block(u)
        if u > 0:
            for peer in cols:
                arrived(acts.at[peer, b], ax_recv.at[u - 1, peer], {"col": peer})

        @pl.loop(0, Q // V)
        def _(j):
            at = pl.ds(pl.multiple_of(j * V, V), V)
            total = contract(acts[0, b], ab[0, :, at], 1, 0)
            for k in range(1, nc):
                total = total + contract(acts[k, b], ab[k, :, at], 1, 0)
            part[b, :, at] = total.astype(half)

        for k, peer in enumerate(rows):
            send(part.at[b, pl.ds(pl.multiple_of(peer * S, 16), S)], precv.at[u, r],
                 rs_send.at[u, k], rs_recv.at[u, r], {"row": peer})

    def reduce_block(u):
        b = tok_block(u)
        at = pl.ds(pl.multiple_of(r * S, 16), S)
        total = part[b, at, :].astype(wide)
        for peer in rows:
            arrived(precv.at[u, peer], rs_recv.at[u, peer], {"row": peer})
            total = total + precv[u, peer].astype(wide)
        act_half[b, at, :] = total.astype(half)
        for k, peer in enumerate(rows):
            piece = act_half.at[b, at]
            send(piece, piece, ag_send.at[u, k], ag_recv.at[u, r], {"row": peer})

    for copy in ab_in:
        copy.wait()
    act_block(0)
    for peer in cols:
        arrived(grecv.at[peer], g_recv.at[peer], {"col": peer})

    @pl.loop(0, Pp // W)
    def _(j):
        at = pl.ds(pl.multiple_of(j * W, W), W)
        total = gown[:, at]
        for peer in cols:
            total = total + grecv[peer, :, at].astype(wide)
        grad_all[c, t, :, at] = (total * total).astype(half)

    ring(grad_all, 0, c_send, c_recv)
    spread(grad_all, 0, nt - 1, cx_send, cx_recv)
    for s in range(1, nt - 1):
        ring_recv(acts, s, a_send, a_recv, ax_send, ax_recv)
        act_block(s)
        ring_recv(grad_all, s - 1, c_send, c_recv, cx_send, cx_recv)
        reduce_block(s - 1)
    act_block(nt - 1)
    ring_recv(grad_all, nt - 2, c_send, c_recv, cx_send, cx_recv)
    reduce_block(nt - 2)
    reduce_block(nt - 1)
    for u in range(nt):
        for peer in rows:
            piece = act_half.at[tok_block(u), pl.ds(pl.multiple_of(peer * S, 16), S)]
            arrived(piece, ag_recv.at[u, peer], {"row": peer})
        for peer in cols:
            slot = (u + nt - 1) % nt
            arrived(grad_all.at[peer, tok_block(u)], cx_recv.at[slot, peer], {"col": peer})
    for copy in sent:
        copy.wait_send()


def output_kernel(nt, nr, nc, hp, gb_hbm, out, xr, zs, zr, hid, gb, osend, orecv,
                  l_sem, x_send, x_recv, z_send, z_recv, h_send, h_recv,
                  rs_send, rs_recv, ag_send, ag_recv):
    R, Pp = hid.shape[1:]
    chunks, _, Oc = osend.shape
    S = R // nr
    gb_in = pltpu.make_async_copy(gb_hbm, gb, l_sem)
    gb_in.start()
    t, r, c = enter(nt, nr, nc)
    right = {"tok": lax.rem(t + 1, nt)}
    cols = [lax.rem(c + k, nc) for k in range(1, nc)]
    rows = [lax.rem(r + k, nr) for k in range(1, nr)]
    sent = []

    def send(*args):
        copy = remote(*args)
        copy.start()
        sent.append(copy)

    def tok_block(u):
        return lax.rem(t - 1 - u + 2 * nt, nt)

    def piece_of(peer):
        return pl.ds(pl.multiple_of(peer * Pp, 128), Pp)

    for u in range(nt):
        for k, peer in enumerate(cols):
            send(hp.at[tok_block(u), :, piece_of(peer)], xr.at[u, c],
                 x_send.at[u, k], x_recv.at[u, c], {"col": peer})
    for u in range(nt):
        b = tok_block(u)
        for peer in cols:
            arrived(xr.at[u, peer], x_recv.at[u, peer], {"col": peer})
        if u > 0:
            arrived(zr.at[u - 1], z_recv.at[u - 1], right)

        @pl.loop(0, R // 32)
        def _(i):
            at = pl.ds(pl.multiple_of(i * 32, 32), 32)
            total = hp[b, at, piece_of(c)].astype(wide)
            for peer in cols:
                total = total + xr[u, peer, at, :].astype(wide)
            if u > 0:
                total = total + zr[u - 1, at, :].astype(wide)
            if u < nt - 1:
                zs[u, at, :] = total.astype(half)
            else:
                hid[c, at, :] = total.astype(half)

        if u < nt - 1:
            send(zs.at[u], zr.at[u], z_send.at[u], z_recv.at[u], right)
    for k, peer in enumerate(cols):
        send(hid.at[c], hid.at[c], h_send.at[k], h_recv.at[c], {"col": peer})
    gb_in.wait()
    for peer in cols:
        arrived(hid.at[peer], h_recv.at[peer], {"col": peer})
    W = min(256, Oc)

    def columns(j):
        return pl.ds(j * Oc, Oc)

    def reduce_chunk(j):
        at = pl.ds(pl.multiple_of(r * S, 16), S)
        total = osend[j, at, :].astype(wide)
        for peer in rows:
            arrived(orecv.at[j, peer], rs_recv.at[j, peer], {"row": peer})
            total = total + orecv[j, peer].astype(wide)
        out[at, columns(j)] = total.astype(half)
        for k, peer in enumerate(rows):
            piece = out.at[at, columns(j)]
            send(piece, piece, ag_send.at[j, k], ag_recv.at[j, r], {"row": peer})

    for j in range(chunks):
        @pl.loop(0, Oc // W)
        def _(i):
            at = pl.ds(pl.multiple_of(j * Oc + i * W, W), W)
            total = contract(hid[0], gb[at, pl.ds(0, Pp)], 1, 1)
            for k in range(1, nc):
                total = total + contract(hid[k], gb[at, pl.ds(k * Pp, Pp)], 1, 1)
            osend[j, :, pl.ds(pl.multiple_of(i * W, W), W)] = total.astype(half)

        for k, peer in enumerate(rows):
            send(osend.at[j, pl.ds(pl.multiple_of(peer * S, 16), S)], orecv.at[j, r],
                 rs_send.at[j, k], rs_recv.at[j, r], {"row": peer})
        if j > 1:
            reduce_chunk(j - 2)
    reduce_chunk(chunks - 2)
    reduce_chunk(chunks - 1)
    for j in range(chunks):
        for peer in rows:
            piece = out.at[pl.ds(pl.multiple_of(peer * S, 16), S), columns(j)]
            arrived(piece, ag_recv.at[j, peer], {"row": peer})
    for copy in sent:
        copy.wait_send()


def project(nt, nr, nc, activations, gradients, act_basis, grad_basis):
    R, F = activations.shape
    Q = act_basis.shape[1]
    G, Pn = grad_basis.shape
    Fp, Pp, S = F // nc, Pn // nc, R // nr
    dma = pltpu.SemaphoreType.DMA
    return pl.pallas_call(
        functools.partial(project_kernel, nt, nr, nc),
        out_shape=(
            jax.ShapeDtypeStruct((nt, R, Q), half),
            jax.ShapeDtypeStruct((nc, nt, R, Pp), half),
        ),
        in_specs=[pl.BlockSpec(memory_space=pl.ANY)] * 4,
        out_specs=[pl.BlockSpec(memory_space=pltpu.VMEM)] * 2,
        scratch_shapes=[
            pltpu.VMEM((nc, nt, R, Fp), half),
            pltpu.VMEM((R, G), half),
            pltpu.VMEM((nc, Fp, Q), half),
            pltpu.VMEM((nc, G, Pp), half),
            pltpu.VMEM((nc, R, Pp), half),
            pltpu.VMEM((R, Pp), wide),
            pltpu.VMEM((nc, R, Pp), half),
            pltpu.VMEM((nt, R, Q), half),
            pltpu.VMEM((nt, nr, S, Q), half),
            dma((3 * nc + 1,)),
            dma((nc,)), dma((nc,)),
            dma((nt,)), dma((nt,)), dma((nt, nc)), dma((nt, nc)),
            dma((nt,)), dma((nt,)), dma((nt, nc)), dma((nt, nc)),
            dma((nt, nr)), dma((nt, nr)), dma((nt, nr)), dma((nt, nr)),
        ],
        compiler_params=pltpu.CompilerParams(
            collective_id=0, has_side_effects=True, vmem_limit_bytes=VMEM_BYTES
        ),
        cost_estimate=pl.CostEstimate(
            flops=2 * R * G * Pn + 2 * nt * R * F * Q, bytes_accessed=2 * (G * Pn + F * Q), transcendentals=0
        ),
    )(activations, gradients, act_basis, grad_basis)


def shift(nt, nr, nc, hidden_part, grad_basis):
    R = hidden_part.shape[1]
    G, Pn = grad_basis.shape
    Pp, S = Pn // nc, R // nr
    chunks = 4
    Oc = G // chunks
    dma = pltpu.SemaphoreType.DMA
    return pl.pallas_call(
        functools.partial(output_kernel, nt, nr, nc),
        out_shape=jax.ShapeDtypeStruct((R, G), half),
        in_specs=[pl.BlockSpec(memory_space=pltpu.VMEM), pl.BlockSpec(memory_space=pl.ANY)],
        out_specs=pl.BlockSpec(memory_space=pltpu.VMEM),
        scratch_shapes=[
            pltpu.VMEM((nt, nc, R, Pp), half),
            pltpu.VMEM((nt, R, Pp), half),
            pltpu.VMEM((nt, R, Pp), half),
            pltpu.VMEM((nc, R, Pp), half),
            pltpu.VMEM((G, Pn), half),
            pltpu.VMEM((chunks, R, Oc), half),
            pltpu.VMEM((chunks, nr, S, Oc), half),
            dma,
            dma((nt, nc)), dma((nt, nc)), dma((nt,)), dma((nt,)), dma((nc,)), dma((nc,)),
            dma((chunks, nr)), dma((chunks, nr)), dma((chunks, nr)), dma((chunks, nr)),
        ],
        compiler_params=pltpu.CompilerParams(
            collective_id=1, has_side_effects=True, vmem_limit_bytes=VMEM_BYTES
        ),
        cost_estimate=pl.CostEstimate(flops=2 * R * G * Pn, bytes_accessed=2 * G * Pn, transcendentals=0),
    )(hidden_part, grad_basis)


def shards(nt, nr, nc, activations, gradients, act_basis, grad_basis, eigen_noise):
    R = activations.shape[0]
    token_count = R * nt
    act_half, grad_all = project(nt, nr, nc, activations, gradients, act_basis, grad_basis)
    act_half = act_half.reshape(token_count, -1)
    act_wide = act_half.astype(wide)
    act_sq = (act_wide * act_wide).astype(half)
    grad_all = grad_all.reshape(nc, token_count, -1)
    scales = lax.dot_general(
        grad_all, act_sq, (((1,), (0,)), ((), ())), preferred_element_type=wide
    ).reshape(eigen_noise.shape) / token_count
    scaled = (eigen_noise * lax.rsqrt(token_count * (scales + damping))).astype(half)
    hidden_part = contract(act_half, scaled, 1, 1).astype(half).reshape(nt, R, -1)
    return (scales, shift(nt, nr, nc, hidden_part, grad_basis))


def solution(mesh):
    in_specs = (
        P("tok", "row"),
        P("tok", "col"),
        P("row", ("tok", "col")),
        P("col", "row"),
        P("row", ("tok", "col")),
    )
    out_specs = (P("row", ("tok", "col")), P("tok", "col"))
    sizes = (mesh.shape["tok"], mesh.shape["row"], mesh.shape["col"])
    return jax.shard_map(
        functools.partial(shards, *sizes), mesh=mesh, in_specs=in_specs, out_specs=out_specs, check_vma=False
    )
```

```python
import functools

import jax
import jax.numpy as jnp
from jax import lax
from jax.experimental import pallas as pl
from jax.experimental.pallas import tpu as pltpu
from jax.sharding import PartitionSpec as P

damping = 0.1
half = jnp.bfloat16
wide = jnp.float32
MESH = pl.DeviceIdType.MESH
VMEM_BYTES = 60 * 1024 * 1024


def contract(former, latter, former_dim, latter_dim):
    return lax.dot_general(
        former,
        latter,
        (((former_dim,), (latter_dim,)), ((), ())),
        preferred_element_type=jnp.float32,
    )


def remote(src, dst, send_sem, recv_sem, where):
    return pltpu.make_async_remote_copy(
        src_ref=src, dst_ref=dst, send_sem=send_sem, recv_sem=recv_sem,
        device_id=where, device_id_type=MESH,
    )


def arrived(ref, sem, where):
    remote(ref, ref, sem, sem, where).wait_recv()


def enter(nt, nr, nc):
    t, r, c = (lax.axis_index(a) for a in ("tok", "row", "col"))
    barrier = pltpu.get_barrier_semaphore()
    places = [{"tok": lax.rem(t + nt - 1, nt)}]
    places += [{"col": lax.rem(c + k, nc)} for k in range(1, nc)]
    places += [{"row": lax.rem(r + k, nr)} for k in range(1, nr)]
    for place in places:
        pl.semaphore_signal(barrier, inc=1, device_id=place, device_id_type=MESH)
    pl.semaphore_wait(barrier, len(places))
    return t, r, c


def project_kernel(nt, nr, nc, act_hbm, grad_hbm, ab_hbm, gb_hbm, act_half, grad_all,
                   acts, grads, ab, gb, gpart, gown, grecv, part, precv,
                   l_sem, g_send, g_recv, a_send, a_recv, az_send, az_recv, ax_send, ax_recv,
                   c_send, c_recv, cx_send, cx_recv, rs_send, rs_recv, ag_send, ag_recv):
    R = grads.shape[0]
    Fp, Q = ab.shape[1:]
    Pp = gb.shape[2]
    S = R // nr
    t0, c0 = lax.axis_index("tok"), lax.axis_index("col")
    locals_ = []

    def local(src, dst):
        copy = pltpu.make_async_copy(src, dst, l_sem.at[len(locals_)])
        copy.start()
        locals_.append(copy)
        return copy

    act_in = [local(act_hbm.at[:, pl.ds(k * Fp, Fp)], acts.at[k, t0]) for k in range(nc)]
    grad_in = local(grad_hbm, grads)
    gb_in = []
    for k in range(nc):
        peer = lax.rem(c0 + k + 1, nc)
        gb_in.append(local(gb_hbm.at[:, pl.ds(pl.multiple_of(peer * Pp, 128), Pp)], gb.at[k]))
    ab_in = [local(ab_hbm.at[pl.ds(k * Fp, Fp), :], ab.at[k]) for k in range(nc)]

    t, r, c = enter(nt, nr, nc)
    right = {"tok": lax.rem(t + 1, nt)}
    cols = [lax.rem(c + k, nc) for k in range(1, nc)]
    rows = [lax.rem(r + k, nr) for k in range(1, nr)]
    sent = []

    def send(*args):
        copy = remote(*args)
        copy.start()
        sent.append(copy)

    def tok_block(s):
        return lax.rem(t - s + nt, nt)

    def ring(buf, s, send_sem, recv_sem):
        piece = buf.at[c, tok_block(s)]
        send(piece, piece, send_sem.at[s], recv_sem.at[s], right)

    def spread(buf, s, slot, send_sem, recv_sem):
        piece = buf.at[c, tok_block(s)]
        for k, peer in enumerate(cols):
            send(piece, piece, send_sem.at[slot, k], recv_sem.at[slot, c], {"col": peer})

    def ring_recv(buf, s, send_sem, recv_sem, x_send, x_recv, skip=False):
        arrived(buf.at[c, tok_block(s + 1)], recv_sem.at[s], right)
        if s < nt - 2:
            ring(buf, s + 1, send_sem, recv_sem)
        if not skip:
            spread(buf, s + 1, s, x_send, x_recv)

    for copy in act_in:
        copy.wait()
    ring(acts, 0, a_send, a_recv)

    W = min(256, Pp)
    grad_in.wait()
    for k, peer in enumerate(cols):
        gb_in[k].wait()

        @pl.loop(0, Pp // W)
        def _(j, k=k, peer=peer):
            at = pl.ds(pl.multiple_of(j * W, W), W)
            gpart[peer, :, at] = contract(grads[...], gb[k, :, at], 1, 0).astype(half)

        send(gpart.at[peer], grecv.at[c], g_send.at[k], g_recv.at[c], {"col": peer})
    for peer in cols:
        send(acts.at[peer, t], acts.at[peer, t], az_send.at[peer], az_recv.at[peer], right)
    ring_recv(acts, 0, a_send, a_recv, ax_send, ax_recv, True)
    gb_in[nc - 1].wait()

    @pl.loop(0, Pp // W)
    def _(j):
        at = pl.ds(pl.multiple_of(j * W, W), W)
        gown[:, at] = contract(grads[...], gb[nc - 1, :, at], 1, 0)

    V = min(256, Q)

    def act_block(u):
        b = tok_block(u)
        if u == 1:
            for peer in cols:
                arrived(acts.at[peer, b], az_recv.at[peer], right)
        if u > 1:
            for peer in cols:
                arrived(acts.at[peer, b], ax_recv.at[u - 1, peer], {"col": peer})

        @pl.loop(0, Q // V)
        def _(j):
            at = pl.ds(pl.multiple_of(j * V, V), V)
            total = contract(acts[0, b], ab[0, :, at], 1, 0)
            for k in range(1, nc):
                total = total + contract(acts[k, b], ab[k, :, at], 1, 0)
            part[b, :, at] = total.astype(half)

        for k, peer in enumerate(rows):
            send(part.at[b, pl.ds(pl.multiple_of(peer * S, 16), S)], precv.at[u, r],
                 rs_send.at[u, k], rs_recv.at[u, r], {"row": peer})

    def reduce_block(u):
        b = tok_block(u)
        at = pl.ds(pl.multiple_of(r * S, 16), S)
        total = part[b, at, :].astype(wide)
        for peer in rows:
            arrived(precv.at[u, peer], rs_recv.at[u, peer], {"row": peer})
            total = total + precv[u, peer].astype(wide)
        act_half[b, at, :] = total.astype(half)
        for k, peer in enumerate(rows):
            piece = act_half.at[b, at]
            send(piece, piece, ag_send.at[u, k], ag_recv.at[u, r], {"row": peer})

    for copy in ab_in:
        copy.wait()
    act_block(0)
    for peer in cols:
        arrived(grecv.at[peer], g_recv.at[peer], {"col": peer})

    @pl.loop(0, Pp // W)
    def _(j):
        at = pl.ds(pl.multiple_of(j * W, W), W)
        total = gown[:, at]
        for peer in cols:
            total = total + grecv[peer, :, at].astype(wide)
        grad_all[c, t, :, at] = (total * total).astype(half)

    ring(grad_all, 0, c_send, c_recv)
    spread(grad_all, 0, nt - 1, cx_send, cx_recv)
    for s in range(1, nt - 1):
        ring_recv(acts, s, a_send, a_recv, ax_send, ax_recv)
        act_block(s)
        ring_recv(grad_all, s - 1, c_send, c_recv, cx_send, cx_recv)
        reduce_block(s - 1)
    act_block(nt - 1)
    ring_recv(grad_all, nt - 2, c_send, c_recv, cx_send, cx_recv)
    reduce_block(nt - 2)
    reduce_block(nt - 1)
    for u in range(nt):
        for peer in rows:
            piece = act_half.at[tok_block(u), pl.ds(pl.multiple_of(peer * S, 16), S)]
            arrived(piece, ag_recv.at[u, peer], {"row": peer})
        for peer in cols:
            slot = (u + nt - 1) % nt
            arrived(grad_all.at[peer, tok_block(u)], cx_recv.at[slot, peer], {"col": peer})
    for copy in sent:
        copy.wait_send()


def output_kernel(nt, nr, nc, act_half, scaled, gb_hbm, out, hp, xr, zs, zr, hid, gb, osend, orecv,
                  l_sem, x_send, x_recv, z_send, z_recv, h_send, h_recv,
                  rs_send, rs_recv, ag_send, ag_recv, fw_send):
    R, Pp = hid.shape[1:]
    chunks, _, Oc = osend.shape
    S = R // nr
    gb_in = pltpu.make_async_copy(gb_hbm, gb, l_sem)
    gb_in.start()
    t, r, c = enter(nt, nr, nc)
    right = {"tok": lax.rem(t + 1, nt)}
    cols = [lax.rem(c + k, nc) for k in range(1, nc)]
    rows = [lax.rem(r + k, nr) for k in range(1, nr)]
    sent = []

    def send(*args):
        copy = remote(*args)
        copy.start()
        sent.append(copy)

    def tok_block(u):
        return lax.rem(t - 1 - u + 2 * nt, nt)

    W = min(256, Pp)

    def hidden_tile(b, piece, j):
        at = pl.ds(pl.multiple_of(piece * Pp + j * W, W), W)
        return contract(act_half[b], scaled[at, :], 1, 1)

    for u in range(nt):
        for k, peer in enumerate(cols):
            @pl.loop(0, Pp // W)
            def _(j, u=u, k=k, peer=peer):
                at = pl.ds(pl.multiple_of(j * W, W), W)
                hp[u, k, :, at] = hidden_tile(tok_block(u), peer, j).astype(half)

            send(hp.at[u, k], xr.at[u, c], x_send.at[u, k], x_recv.at[u, c], {"col": peer})
    for u in range(nt):
        b = tok_block(u)
        for peer in cols:
            arrived(xr.at[u, peer], x_recv.at[u, peer], {"col": peer})
        if u > 0:
            arrived(zr.at[u - 1], z_recv.at[u - 1], right)

        @pl.loop(0, Pp // W)
        def _(j, u=u, b=b):
            at = pl.ds(pl.multiple_of(j * W, W), W)
            total = hidden_tile(b, c, j)
            for peer in cols:
                total = total + xr[u, peer, :, at].astype(wide)
            if u > 0:
                total = total + zr[u - 1, :, at].astype(wide)
            if u < nt - 1:
                zs[u, :, at] = total.astype(half)
            else:
                hid[c, :, at] = total.astype(half)

        if u < nt - 1:
            send(zs.at[u], zr.at[u], z_send.at[u], z_recv.at[u], right)
    for k, peer in enumerate(cols):
        send(hid.at[c], hid.at[c], h_send.at[k], h_recv.at[c], {"col": peer})
    gb_in.wait()
    for peer in cols:
        arrived(hid.at[peer], h_recv.at[peer], {"col": peer})
    V = min(256, Oc)
    twin = r + 1 - 2 * lax.rem(r, 2)
    far = [lax.rem(r + 2 * k, nr) for k in range(1, nr // 2)]

    def columns(j):
        return pl.ds(j * Oc, Oc)

    def reduce_chunk(j):
        at = pl.ds(pl.multiple_of(r * S, 16), S)
        total = osend[j, at, :].astype(wide)
        for peer in rows:
            arrived(orecv.at[j, peer], rs_recv.at[j, peer], {"row": peer})
            total = total + orecv[j, peer].astype(wide)
        out[at, columns(j)] = total.astype(half)
        for k, peer in enumerate(far + [twin]):
            piece = out.at[at, columns(j)]
            send(piece, piece, ag_send.at[j, k], ag_recv.at[j, r], {"row": peer})

    def forward_chunk(j):
        for k, peer in enumerate(far):
            piece = out.at[pl.ds(pl.multiple_of(peer * S, 16), S), columns(j)]
            arrived(piece, ag_recv.at[j, peer], {"row": peer})
            send(piece, piece, fw_send.at[j, k], ag_recv.at[j, peer], {"row": twin})

    for j in range(chunks):
        @pl.loop(0, Oc // V)
        def _(i, j=j):
            at = pl.ds(pl.multiple_of(j * Oc + i * V, V), V)
            total = contract(hid[0], gb[at, pl.ds(0, Pp)], 1, 1)
            for k in range(1, nc):
                total = total + contract(hid[k], gb[at, pl.ds(k * Pp, Pp)], 1, 1)
            osend[j, :, pl.ds(pl.multiple_of(i * V, V), V)] = total.astype(half)

        for k, peer in enumerate(rows):
            send(osend.at[j, pl.ds(pl.multiple_of(peer * S, 16), S)], orecv.at[j, r],
                 rs_send.at[j, k], rs_recv.at[j, r], {"row": peer})
        if j > 1:
            reduce_chunk(j - 2)
    reduce_chunk(chunks - 2)
    for j in range(chunks - 2):
        forward_chunk(j)
    reduce_chunk(chunks - 1)
    forward_chunk(chunks - 2)
    forward_chunk(chunks - 1)
    for j in range(chunks):
        for peer in [twin] + [lax.rem(twin + 2 * k, nr) for k in range(1, nr // 2)]:
            piece = out.at[pl.ds(pl.multiple_of(peer * S, 16), S), columns(j)]
            arrived(piece, ag_recv.at[j, peer], {"row": peer})
    for copy in sent:
        copy.wait_send()


def project(nt, nr, nc, activations, gradients, act_basis, grad_basis):
    R, F = activations.shape
    Q = act_basis.shape[1]
    G, Pn = grad_basis.shape
    Fp, Pp, S = F // nc, Pn // nc, R // nr
    dma = pltpu.SemaphoreType.DMA
    return pl.pallas_call(
        functools.partial(project_kernel, nt, nr, nc),
        out_shape=(
            jax.ShapeDtypeStruct((nt, R, Q), half),
            jax.ShapeDtypeStruct((nc, nt, R, Pp), half),
        ),
        in_specs=[pl.BlockSpec(memory_space=pl.ANY)] * 4,
        out_specs=[pl.BlockSpec(memory_space=pltpu.VMEM)] * 2,
        scratch_shapes=[
            pltpu.VMEM((nc, nt, R, Fp), half),
            pltpu.VMEM((R, G), half),
            pltpu.VMEM((nc, Fp, Q), half),
            pltpu.VMEM((nc, G, Pp), half),
            pltpu.VMEM((nc, R, Pp), half),
            pltpu.VMEM((R, Pp), wide),
            pltpu.VMEM((nc, R, Pp), half),
            pltpu.VMEM((nt, R, Q), half),
            pltpu.VMEM((nt, nr, S, Q), half),
            dma((3 * nc + 1,)),
            dma((nc,)), dma((nc,)),
            dma((nt,)), dma((nt,)), dma((nc,)), dma((nc,)), dma((nt, nc)), dma((nt, nc)),
            dma((nt,)), dma((nt,)), dma((nt, nc)), dma((nt, nc)),
            dma((nt, nr)), dma((nt, nr)), dma((nt, nr)), dma((nt, nr)),
        ],
        compiler_params=pltpu.CompilerParams(
            collective_id=0, has_side_effects=True, vmem_limit_bytes=VMEM_BYTES
        ),
        cost_estimate=pl.CostEstimate(
            flops=2 * R * G * Pn + 2 * nt * R * F * Q, bytes_accessed=2 * (G * Pn + F * Q), transcendentals=0
        ),
    )(activations, gradients, act_basis, grad_basis)


def scale_kernel(token_count, grad, act_half, noise, scales, scaled, act_sq):
    @pl.when((pl.program_id(0) == 0) & (pl.program_id(1) == 0))
    def _():
        value = act_half[...].astype(wide)
        act_sq[...] = (value * value).astype(half)

    total = contract(grad[0], act_sq[...], 0, 0) / token_count
    scales[...] = total
    scaled[...] = (noise[...] * lax.rsqrt(token_count * (total + damping))).astype(half)


def scale(act_half, grad_all, noise):
    Pn, Q = noise.shape
    nc, tokens, Pp = grad_all.shape
    W = min(256, Pp)
    steps = Pp // W
    strip = pl.BlockSpec((W, Q), lambda c, j: (c * steps + j, 0))
    return pl.pallas_call(
        functools.partial(scale_kernel, tokens),
        grid=(nc, steps),
        out_shape=(jax.ShapeDtypeStruct((Pn, Q), wide), jax.ShapeDtypeStruct((Pn, Q), half)),
        in_specs=[
            pl.BlockSpec((1, tokens, W), lambda c, j: (c, 0, j)),
            pl.BlockSpec((tokens, Q), lambda c, j: (0, 0)),
            strip,
        ],
        out_specs=[strip, strip],
        scratch_shapes=[pltpu.VMEM((tokens, Q), half)],
        compiler_params=pltpu.CompilerParams(vmem_limit_bytes=VMEM_BYTES),
        cost_estimate=pl.CostEstimate(
            flops=2 * tokens * Pn * Q, bytes_accessed=10 * Pn * Q, transcendentals=Pn * Q
        ),
    )(grad_all, act_half, noise)


def shift(nt, nr, nc, act_half, scaled, grad_basis):
    R = act_half.shape[1]
    G, Pn = grad_basis.shape
    Pp, S = Pn // nc, R // nr
    chunks = 4
    Oc = G // chunks
    dma = pltpu.SemaphoreType.DMA
    return pl.pallas_call(
        functools.partial(output_kernel, nt, nr, nc),
        out_shape=jax.ShapeDtypeStruct((R, G), half),
        in_specs=[pl.BlockSpec(memory_space=pltpu.VMEM)] * 2 + [pl.BlockSpec(memory_space=pl.ANY)],
        out_specs=pl.BlockSpec(memory_space=pltpu.VMEM),
        scratch_shapes=[
            pltpu.VMEM((nt, nc - 1, R, Pp), half),
            pltpu.VMEM((nt, nc, R, Pp), half),
            pltpu.VMEM((nt, R, Pp), half),
            pltpu.VMEM((nt, R, Pp), half),
            pltpu.VMEM((nc, R, Pp), half),
            pltpu.VMEM((G, Pn), half),
            pltpu.VMEM((chunks, R, Oc), half),
            pltpu.VMEM((chunks, nr, S, Oc), half),
            dma,
            dma((nt, nc)), dma((nt, nc)), dma((nt,)), dma((nt,)), dma((nc,)), dma((nc,)),
            dma((chunks, nr)), dma((chunks, nr)), dma((chunks, nr)), dma((chunks, nr)), dma((chunks, nr)),
        ],
        compiler_params=pltpu.CompilerParams(
            collective_id=1, has_side_effects=True, vmem_limit_bytes=VMEM_BYTES
        ),
        cost_estimate=pl.CostEstimate(flops=2 * R * G * Pn, bytes_accessed=2 * G * Pn, transcendentals=0),
    )(act_half, scaled, grad_basis)


def shards(nt, nr, nc, activations, gradients, act_basis, grad_basis, eigen_noise):
    token_count = activations.shape[0] * nt
    act_half, grad_all = project(nt, nr, nc, activations, gradients, act_basis, grad_basis)
    grad_all = grad_all.reshape(nc, token_count, -1)
    scales, scaled = scale(act_half.reshape(token_count, -1), grad_all, eigen_noise)
    return (scales, shift(nt, nr, nc, act_half, scaled, grad_basis))


def solution(mesh):
    in_specs = (
        P("tok", "row"),
        P("tok", "col"),
        P("row", ("tok", "col")),
        P("col", "row"),
        P("row", ("tok", "col")),
    )
    out_specs = (P("row", ("tok", "col")), P("tok", "col"))
    sizes = (mesh.shape["tok"], mesh.shape["row"], mesh.shape["col"])
    return jax.shard_map(
        functools.partial(shards, *sizes), mesh=mesh, in_specs=in_specs, out_specs=out_specs, check_vma=False
    )
```

```python
import functools

import jax
import jax.numpy as jnp
from jax import lax
from jax.experimental import pallas as pl
from jax.experimental.pallas import tpu as pltpu
from jax.sharding import PartitionSpec as P

damping = 0.1
half = jnp.bfloat16
wide = jnp.float32
MESH = pl.DeviceIdType.MESH
VMEM_BYTES = 60 * 1024 * 1024


def contract(former, latter, former_dim, latter_dim):
    return lax.dot_general(
        former,
        latter,
        (((former_dim,), (latter_dim,)), ((), ())),
        preferred_element_type=jnp.float32,
    )


def remote(src, dst, send_sem, recv_sem, where):
    return pltpu.make_async_remote_copy(
        src_ref=src, dst_ref=dst, send_sem=send_sem, recv_sem=recv_sem,
        device_id=where, device_id_type=MESH,
    )


def arrived(ref, sem, where):
    remote(ref, ref, sem, sem, where).wait_recv()


def enter(nt, nr, nc):
    t, r, c = (lax.axis_index(a) for a in ("tok", "row", "col"))
    barrier = pltpu.get_barrier_semaphore()
    places = [{"tok": lax.rem(t + nt - 1, nt)}]
    places += [{"col": lax.rem(c + k, nc)} for k in range(1, nc)]
    places += [{"row": lax.rem(r + k, nr)} for k in range(1, nr)]
    for place in places:
        pl.semaphore_signal(barrier, inc=1, device_id=place, device_id_type=MESH)
    pl.semaphore_wait(barrier, len(places))
    return t, r, c


def project_kernel(nt, nr, nc, act_hbm, grad_hbm, ab_hbm, gb_hbm, act_half, grad_all,
                   acts, grads, ab, gb, gpart, gown, grecv, part, precv,
                   l_sem, g_send, g_recv, a_send, a_recv, az_send, az_recv, ax_send, ax_recv,
                   c_send, c_recv, cx_send, cx_recv, rs_send, rs_recv, ag_send, ag_recv):
    R = grads.shape[0]
    Fp, Q = ab.shape[1:]
    Pp = gb.shape[2]
    S = R // nr
    Wp = gown.shape[2]
    H = Pp // Wp
    t0, c0 = lax.axis_index("tok"), lax.axis_index("col")
    locals_ = []

    def local(src, dst):
        copy = pltpu.make_async_copy(src, dst, l_sem.at[len(locals_)])
        copy.start()
        locals_.append(copy)
        return copy

    act_in = [local(act_hbm.at[:, pl.ds(k * Fp, Fp)], acts.at[k, t0]) for k in range(nc)]
    grad_in = local(grad_hbm, grads)
    gb_in = []
    for k in range(nc):
        peer = lax.rem(c0 + k + 1, nc)
        gb_in.append(local(gb_hbm.at[:, pl.ds(pl.multiple_of(peer * Pp, 128), Pp)], gb.at[k]))
    ab_in = [local(ab_hbm.at[pl.ds(k * Fp, Fp), :], ab.at[k]) for k in range(nc)]

    t, r, c = enter(nt, nr, nc)
    right = {"tok": lax.rem(t + 1, nt)}
    cols = [lax.rem(c + k, nc) for k in range(1, nc)]
    rows = [lax.rem(r + k, nr) for k in range(1, nr)]
    sent = []

    def send(*args):
        copy = remote(*args)
        copy.start()
        sent.append(copy)

    def tok_block(s):
        return lax.rem(t - s + nt, nt)

    def ring(buf, s, send_sem, recv_sem, h=0, H=1):
        piece = buf.at[c * H + h, tok_block(s)]
        send(piece, piece, send_sem.at[s * H + h], recv_sem.at[s * H + h], right)

    def spread(buf, s, slot, send_sem, recv_sem, h=0, H=1):
        piece = buf.at[c * H + h, tok_block(s)]
        for k, peer in enumerate(cols):
            send(piece, piece, send_sem.at[slot * H + h, k], recv_sem.at[slot * H + h, c], {"col": peer})

    def ring_recv(buf, s, send_sem, recv_sem, x_send, x_recv, skip=False, h=0, H=1):
        arrived(buf.at[c * H + h, tok_block(s + 1)], recv_sem.at[s * H + h], right)
        if s < nt - 2:
            ring(buf, s + 1, send_sem, recv_sem, h, H)
        if not skip:
            spread(buf, s + 1, s, x_send, x_recv, h, H)

    def squares_recv(s):
        for h in range(H):
            ring_recv(grad_all, s, c_send, c_recv, cx_send, cx_recv, h=h, H=H)

    for copy in act_in:
        copy.wait()
    ring(acts, 0, a_send, a_recv)

    W = min(256, Wp)
    grad_in.wait()
    for k, peer in enumerate(cols):
        gb_in[k].wait()
        for h in range(H):
            @pl.loop(0, Wp // W)
            def _(j, k=k, peer=peer, h=h):
                at = pl.ds(pl.multiple_of(j * W, W), W)
                tile = gb[k, :, pl.ds(pl.multiple_of(h * Wp + j * W, W), W)]
                gpart[peer * H + h, :, at] = contract(grads[...], tile, 1, 0).astype(half)

            send(gpart.at[peer * H + h], grecv.at[c * H + h],
                 g_send.at[k * H + h], g_recv.at[c * H + h], {"col": peer})
    for peer in cols:
        send(acts.at[peer, t], acts.at[peer, t], az_send.at[peer], az_recv.at[peer], right)
    ring_recv(acts, 0, a_send, a_recv, ax_send, ax_recv, True)
    gb_in[nc - 1].wait()

    for h in range(H):
        @pl.loop(0, Wp // W)
        def _(j, h=h):
            at = pl.ds(pl.multiple_of(j * W, W), W)
            tile = gb[nc - 1, :, pl.ds(pl.multiple_of(h * Wp + j * W, W), W)]
            gown[h, :, at] = contract(grads[...], tile, 1, 0)

    V = min(256, Q)

    def act_block(u):
        b = tok_block(u)
        if u == 1:
            for peer in cols:
                arrived(acts.at[peer, b], az_recv.at[peer], right)
        if u > 1:
            for peer in cols:
                arrived(acts.at[peer, b], ax_recv.at[u - 1, peer], {"col": peer})

        @pl.loop(0, Q // V)
        def _(j):
            at = pl.ds(pl.multiple_of(j * V, V), V)
            total = contract(acts[0, b], ab[0, :, at], 1, 0)
            for k in range(1, nc):
                total = total + contract(acts[k, b], ab[k, :, at], 1, 0)
            part[b, :, at] = total.astype(half)

        for k, peer in enumerate(rows):
            send(part.at[b, pl.ds(pl.multiple_of(peer * S, 16), S)], precv.at[u, r],
                 rs_send.at[u, k], rs_recv.at[u, r], {"row": peer})

    def reduce_block(u):
        b = tok_block(u)
        at = pl.ds(pl.multiple_of(r * S, 16), S)
        total = part[b, at, :].astype(wide)
        for peer in rows:
            arrived(precv.at[u, peer], rs_recv.at[u, peer], {"row": peer})
            total = total + precv[u, peer].astype(wide)
        act_half[b, at, :] = total.astype(half)
        for k, peer in enumerate(rows):
            piece = act_half.at[b, at]
            send(piece, piece, ag_send.at[u, k], ag_recv.at[u, r], {"row": peer})

    for copy in ab_in:
        copy.wait()
    for h in range(H):
        for peer in cols:
            arrived(grecv.at[peer * H + h], g_recv.at[peer * H + h], {"col": peer})

        @pl.loop(0, Wp // W)
        def _(j, h=h):
            at = pl.ds(pl.multiple_of(j * W, W), W)
            total = gown[h, :, at]
            for peer in cols:
                total = total + grecv[peer * H + h, :, at].astype(wide)
            grad_all[c * H + h, t, :, at] = (total * total).astype(half)

        ring(grad_all, 0, c_send, c_recv, h, H)
        spread(grad_all, 0, nt - 1, cx_send, cx_recv, h, H)
    act_block(0)
    for s in range(1, nt - 1):
        ring_recv(acts, s, a_send, a_recv, ax_send, ax_recv)
        act_block(s)
        squares_recv(s - 1)
        reduce_block(s - 1)
    act_block(nt - 1)
    squares_recv(nt - 2)
    reduce_block(nt - 2)
    reduce_block(nt - 1)
    for u in range(nt):
        for peer in rows:
            piece = act_half.at[tok_block(u), pl.ds(pl.multiple_of(peer * S, 16), S)]
            arrived(piece, ag_recv.at[u, peer], {"row": peer})
        for peer in cols:
            slot = (u + nt - 1) % nt
            for h in range(H):
                piece = grad_all.at[peer * H + h, tok_block(u)]
                arrived(piece, cx_recv.at[slot * H + h, peer], {"col": peer})
    for copy in sent:
        copy.wait_send()


def output_kernel(nt, nr, nc, act_half, scaled, gb_hbm, out, hp, xr, zs, zr, hid, gb, osend, orecv,
                  l_sem, x_send, x_recv, z_send, z_recv, h_send, h_recv,
                  rs_send, rs_recv, ag_send, ag_recv, fw_send):
    R, Wp = hid.shape[1:]
    H = hid.shape[0] // nc
    Pp = H * Wp
    chunks, _, Oc = osend.shape
    S = R // nr
    gb_in = pltpu.make_async_copy(gb_hbm, gb, l_sem)
    gb_in.start()
    t, r, c = enter(nt, nr, nc)
    right = {"tok": lax.rem(t + 1, nt)}
    cols = [lax.rem(c + k, nc) for k in range(1, nc)]
    rows = [lax.rem(r + k, nr) for k in range(1, nr)]
    sent = []

    def send(*args):
        copy = remote(*args)
        copy.start()
        sent.append(copy)

    def tok_block(u):
        return lax.rem(t - 1 - u + 2 * nt, nt)

    W = min(256, Wp)

    def hidden_tile(b, start, j):
        at = pl.ds(pl.multiple_of(start + j * W, W), W)
        return contract(act_half[b], scaled[at, :], 1, 1)

    steps = [(u, h) for u in range(nt) for h in range(H)]
    for v, (u, h) in enumerate(steps):
        for k, peer in enumerate(cols):
            @pl.loop(0, Wp // W)
            def _(j, u=u, v=v, h=h, k=k, peer=peer):
                at = pl.ds(pl.multiple_of(j * W, W), W)
                hp[v, k, :, at] = hidden_tile(tok_block(u), peer * Pp + h * Wp, j).astype(half)

            send(hp.at[v, k], xr.at[v, c], x_send.at[v, k], x_recv.at[v, c], {"col": peer})
    for v, (u, h) in enumerate(steps):
        for peer in cols:
            arrived(xr.at[v, peer], x_recv.at[v, peer], {"col": peer})
        if u > 0:
            arrived(zr.at[v - H], z_recv.at[v - H], right)

        @pl.loop(0, Wp // W)
        def _(j, u=u, v=v, h=h):
            at = pl.ds(pl.multiple_of(j * W, W), W)
            total = hidden_tile(tok_block(u), c * Pp + h * Wp, j)
            for peer in cols:
                total = total + xr[v, peer, :, at].astype(wide)
            if u > 0:
                total = total + zr[v - H, :, at].astype(wide)
            if u < nt - 1:
                zs[v, :, at] = total.astype(half)
            else:
                hid[c * H + h, :, at] = total.astype(half)

        if u < nt - 1:
            send(zs.at[v], zr.at[v], z_send.at[v], z_recv.at[v], right)
        else:
            for k, peer in enumerate(cols):
                piece = hid.at[c * H + h]
                send(piece, piece, h_send.at[h, k], h_recv.at[c * H + h], {"col": peer})
    gb_in.wait()
    for h in range(H):
        for peer in cols:
            arrived(hid.at[peer * H + h], h_recv.at[peer * H + h], {"col": peer})
    V = min(256, Oc)
    twin = r + 1 - 2 * lax.rem(r, 2)
    far = [lax.rem(r + 2 * k, nr) for k in range(1, nr // 2)]

    def columns(j):
        return pl.ds(j * Oc, Oc)

    def reduce_chunk(j):
        at = pl.ds(pl.multiple_of(r * S, 16), S)
        total = osend[j, at, :].astype(wide)
        for peer in rows:
            arrived(orecv.at[j, peer], rs_recv.at[j, peer], {"row": peer})
            total = total + orecv[j, peer].astype(wide)
        out[at, columns(j)] = total.astype(half)
        for k, peer in enumerate(far + [twin]):
            piece = out.at[at, columns(j)]
            send(piece, piece, ag_send.at[j, k], ag_recv.at[j, r], {"row": peer})

    def forward_chunk(j):
        for k, peer in enumerate(far):
            piece = out.at[pl.ds(pl.multiple_of(peer * S, 16), S), columns(j)]
            arrived(piece, ag_recv.at[j, peer], {"row": peer})
            send(piece, piece, fw_send.at[j, k], ag_recv.at[j, peer], {"row": twin})

    for j in range(chunks):
        @pl.loop(0, Oc // V)
        def _(i, j=j):
            at = pl.ds(pl.multiple_of(j * Oc + i * V, V), V)
            total = contract(hid[0], gb[at, pl.ds(0, Wp)], 1, 1)
            for k in range(1, nc * H):
                total = total + contract(hid[k], gb[at, pl.ds(k * Wp, Wp)], 1, 1)
            osend[j, :, pl.ds(pl.multiple_of(i * V, V), V)] = total.astype(half)

        for k, peer in enumerate(rows):
            send(osend.at[j, pl.ds(pl.multiple_of(peer * S, 16), S)], orecv.at[j, r],
                 rs_send.at[j, k], rs_recv.at[j, r], {"row": peer})
        if j > 1:
            reduce_chunk(j - 2)
    reduce_chunk(chunks - 2)
    for j in range(chunks - 2):
        forward_chunk(j)
    reduce_chunk(chunks - 1)
    forward_chunk(chunks - 2)
    forward_chunk(chunks - 1)
    for j in range(chunks):
        for peer in [twin] + [lax.rem(twin + 2 * k, nr) for k in range(1, nr // 2)]:
            piece = out.at[pl.ds(pl.multiple_of(peer * S, 16), S), columns(j)]
            arrived(piece, ag_recv.at[j, peer], {"row": peer})
    for copy in sent:
        copy.wait_send()


def halves(extent):
    return 2 if extent >= 512 else 1


def project(nt, nr, nc, activations, gradients, act_basis, grad_basis):
    R, F = activations.shape
    Q = act_basis.shape[1]
    G, Pn = grad_basis.shape
    Fp, Pp, S = F // nc, Pn // nc, R // nr
    H = halves(Pp)
    Wp = Pp // H
    dma = pltpu.SemaphoreType.DMA
    return pl.pallas_call(
        functools.partial(project_kernel, nt, nr, nc),
        out_shape=(
            jax.ShapeDtypeStruct((nt, R, Q), half),
            jax.ShapeDtypeStruct((nc * H, nt, R, Wp), half),
        ),
        in_specs=[pl.BlockSpec(memory_space=pl.ANY)] * 4,
        out_specs=[pl.BlockSpec(memory_space=pltpu.VMEM)] * 2,
        scratch_shapes=[
            pltpu.VMEM((nc, nt, R, Fp), half),
            pltpu.VMEM((R, G), half),
            pltpu.VMEM((nc, Fp, Q), half),
            pltpu.VMEM((nc, G, Pp), half),
            pltpu.VMEM((nc * H, R, Wp), half),
            pltpu.VMEM((H, R, Wp), wide),
            pltpu.VMEM((nc * H, R, Wp), half),
            pltpu.VMEM((nt, R, Q), half),
            pltpu.VMEM((nt, nr, S, Q), half),
            dma((3 * nc + 1,)),
            dma((nc * H,)), dma((nc * H,)),
            dma((nt,)), dma((nt,)), dma((nc,)), dma((nc,)), dma((nt, nc)), dma((nt, nc)),
            dma((nt * H,)), dma((nt * H,)), dma((nt * H, nc)), dma((nt * H, nc)),
            dma((nt, nr)), dma((nt, nr)), dma((nt, nr)), dma((nt, nr)),
        ],
        compiler_params=pltpu.CompilerParams(
            collective_id=0, has_side_effects=True, vmem_limit_bytes=VMEM_BYTES
        ),
        cost_estimate=pl.CostEstimate(
            flops=2 * R * G * Pn + 2 * nt * R * F * Q, bytes_accessed=2 * (G * Pn + F * Q), transcendentals=0
        ),
    )(activations, gradients, act_basis, grad_basis)


def scale_kernel(token_count, grad, act_half, noise, scales, scaled, act_sq):
    @pl.when((pl.program_id(0) == 0) & (pl.program_id(1) == 0))
    def _():
        value = act_half[...].astype(wide)
        act_sq[...] = (value * value).astype(half)

    total = contract(grad[0], act_sq[...], 0, 0) / token_count
    scales[...] = total
    scaled[...] = (noise[...] * lax.rsqrt(token_count * (total + damping))).astype(half)


def scale(act_half, grad_all, noise):
    Pn, Q = noise.shape
    nc, tokens, Pp = grad_all.shape
    W = min(256, Pp)
    steps = Pp // W
    strip = pl.BlockSpec((W, Q), lambda c, j: (c * steps + j, 0))
    return pl.pallas_call(
        functools.partial(scale_kernel, tokens),
        grid=(nc, steps),
        out_shape=(jax.ShapeDtypeStruct((Pn, Q), wide), jax.ShapeDtypeStruct((Pn, Q), half)),
        in_specs=[
            pl.BlockSpec((1, tokens, W), lambda c, j: (c, 0, j)),
            pl.BlockSpec((tokens, Q), lambda c, j: (0, 0)),
            strip,
        ],
        out_specs=[strip, strip],
        scratch_shapes=[pltpu.VMEM((tokens, Q), half)],
        compiler_params=pltpu.CompilerParams(vmem_limit_bytes=VMEM_BYTES),
        cost_estimate=pl.CostEstimate(
            flops=2 * tokens * Pn * Q, bytes_accessed=10 * Pn * Q, transcendentals=Pn * Q
        ),
    )(grad_all, act_half, noise)


def shift(nt, nr, nc, act_half, scaled, grad_basis):
    R = act_half.shape[1]
    G, Pn = grad_basis.shape
    Pp, S = Pn // nc, R // nr
    H = halves(Pp)
    Wp = Pp // H
    chunks = 8
    Oc = G // chunks
    dma = pltpu.SemaphoreType.DMA
    return pl.pallas_call(
        functools.partial(output_kernel, nt, nr, nc),
        out_shape=jax.ShapeDtypeStruct((R, G), half),
        in_specs=[pl.BlockSpec(memory_space=pltpu.VMEM)] * 2 + [pl.BlockSpec(memory_space=pl.ANY)],
        out_specs=pl.BlockSpec(memory_space=pltpu.VMEM),
        scratch_shapes=[
            pltpu.VMEM((nt * H, nc - 1, R, Wp), half),
            pltpu.VMEM((nt * H, nc, R, Wp), half),
            pltpu.VMEM((nt * H, R, Wp), half),
            pltpu.VMEM((nt * H, R, Wp), half),
            pltpu.VMEM((nc * H, R, Wp), half),
            pltpu.VMEM((G, Pn), half),
            pltpu.VMEM((chunks, R, Oc), half),
            pltpu.VMEM((chunks, nr, S, Oc), half),
            dma,
            dma((nt * H, nc)), dma((nt * H, nc)), dma((nt * H,)), dma((nt * H,)), dma((H, nc)), dma((nc * H,)),
            dma((chunks, nr)), dma((chunks, nr)), dma((chunks, nr)), dma((chunks, nr)), dma((chunks, nr)),
        ],
        compiler_params=pltpu.CompilerParams(
            collective_id=1, has_side_effects=True, vmem_limit_bytes=VMEM_BYTES
        ),
        cost_estimate=pl.CostEstimate(flops=2 * R * G * Pn, bytes_accessed=2 * G * Pn, transcendentals=0),
    )(act_half, scaled, grad_basis)


def shards(nt, nr, nc, activations, gradients, act_basis, grad_basis, eigen_noise):
    token_count = activations.shape[0] * nt
    act_half, grad_all = project(nt, nr, nc, activations, gradients, act_basis, grad_basis)
    grad_all = grad_all.reshape(grad_all.shape[0], token_count, -1)
    scales, scaled = scale(act_half.reshape(token_count, -1), grad_all, eigen_noise)
    return (scales, shift(nt, nr, nc, act_half, scaled, grad_basis))


def solution(mesh):
    in_specs = (
        P("tok", "row"),
        P("tok", "col"),
        P("row", ("tok", "col")),
        P("col", "row"),
        P("row", ("tok", "col")),
    )
    out_specs = (P("row", ("tok", "col")), P("tok", "col"))
    sizes = (mesh.shape["tok"], mesh.shape["row"], mesh.shape["col"])
    return jax.shard_map(
        functools.partial(shards, *sizes), mesh=mesh, in_specs=in_specs, out_specs=out_specs, check_vma=False
    )
```
